128 devices in a mesh: kv: 32 (over y, x, core), head: 4 (over z).
Axes of the slice: x: 4, y: 4, z: 4, core: 2. Of those that a mesh axis runs over, the one named last changes fastest.
Arguments:
- queries: bfloat16 [8, 16384], P(None, 'head'), may hold values from -9 to 9
- kv_cache: bfloat16 [8, 16384, 2, 1024], P(None, 'kv', None, 'head'), may hold values from -12 to 12
- new_kv: bfloat16 [8, 2, 1024], P(None, None, 'head'), may hold values from -12 to 12
- offsets: int32 [8], replicated, may hold values from 0 to 31, as said below
- lengths: int32 [8], replicated, may hold values from 4096 to 16384, as said below
- residual: bfloat16 [8, 16384], P(None, ('kv', 'head')), may hold values from -6 to 6
- out_weight: bfloat16 [16384, 16384], P('head', 'kv'), may hold values from -0.046875 to 0.046875
- norm_gain: bfloat16 [16384], P(('kv', 'head')), may hold values from 0.099609375 to 1.8984375
- gate_weight: bfloat16 [16384, 32768], P(None, ('kv', 'head')), may hold values from -0.046875 to 0.046875
- up_weight: bfloat16 [16384, 32768], P(None, ('kv', 'head')), may hold values from -0.046875 to 0.046875
Outputs:
- stream: bfloat16 [8, 16384], P(None, ('kv', 'head'))
- gated: bfloat16 [8, 32768], P(None, ('kv', 'head'))
The draws below stay inside these ranges and needn't reach their ends.
Inputs may be any that keep to these rules, and one draw needn't show every extreme that they name: Position p of sequence b sits on kv index (offsets[b] + p // 512) mod 32, slot p mod 512 there. `lengths`: in every draw some sequence fills all 16384 slots.
All inputs are finite; a program needn't handle non-finite values.
Results may differ from the reference program's by a relative error of at most 0.04.
Values may be sent and summed in bfloat16 or wider, within the bound.
No kernel may reach another device: no remote copies, remote signals or barrier semaphores. Data moves between devices by JAX's collectives and lax.ppermute only.
A program may use at most 128 MiB of HBM per device.

```python
import jax
import jax.numpy as jnp
from jax import lax

D = 16384
H = 128
KVH = 8
HD = 128
FF_WIN = 32768
ROWS = 8
S_DEV = 512
KV_SHARDS = 32
SEQ = 16384


def shared_offsets(key):
    return jax.random.randint(jax.random.fold_in(key, 71), (ROWS,), 0, KV_SHARDS).astype(jnp.int32)


def draw_offsets(key, part):
    return shared_offsets(key)


def draw_lengths(key, part):
    key = jax.random.fold_in(key, 5)
    first_key, second_key = jax.random.split(key)
    drawn = jax.random.randint(first_key, (ROWS,), SEQ // 4, SEQ + 1)
    longest = jax.random.randint(second_key, (), 0, ROWS)
    drawn = jnp.where(jnp.arange(ROWS) == longest, SEQ, drawn)
    return drawn.astype(jnp.int32)


def draw_kv_cache(key, part):
    key = jax.random.fold_in(key, 7)
    cache = jnp.clip(jax.random.normal(key, (ROWS, SEQ, 2, KVH * HD), jnp.float32) * 2.0, -12.0, 12.0)
    return cache.astype(jnp.bfloat16)


def draw_queries(key, part):
    key = jax.random.fold_in(key, 11)
    drawn = jnp.clip(jax.random.normal(key, (ROWS, H * HD), jnp.float32) * 1.5, -9.0, 9.0)
    return drawn.astype(jnp.bfloat16)


def steps_of(rng, shape, cuts, low, largest):
    def one(position, blocks):
        draws = jax.random.uniform(jax.random.fold_in(jax.random.fold_in(rng, 6), position), (blocks,), jnp.float32, low / len(cuts), largest / len(cuts))
        return jnp.repeat(jnp.exp(draws), shape[position] // blocks).reshape((-1,) + (1,) * (len(shape) - position - 1))

    gain = one(*cuts[0])
    for cut in cuts[1:]:
        gain = gain * one(*cut)
    return gain


def centred(rng, shape, spread, most, cuts=(), held_as=jnp.bfloat16):
    values = spread * jax.random.normal(rng, shape, jnp.float32)
    if cuts:
        values = values * steps_of(rng, shape, cuts, -0.22, 0.18)
    return jnp.clip(values, -most, most).astype(held_as)


def setup_inputs(seed: int = 0) -> dict:
    key_of = jax.random.split(jax.random.key(seed), 11)
    queries = draw_queries(jax.random.fold_in(key_of[10], 71), 0)
    kv_cache = draw_kv_cache(jax.random.fold_in(key_of[10], 71), 0)
    new_kv = centred(key_of[2], (ROWS, 2, KVH * HD), 2.0, 12.0, ((2, 4),))
    offsets = draw_offsets(jax.random.fold_in(key_of[10], 71), 0)
    lengths = draw_lengths(jax.random.fold_in(key_of[10], 71), 0)
    residual = centred(key_of[5], (ROWS, D), 1.0, 6.0, ((1, 128),))
    out_weight = centred(key_of[6], (H * HD, D), (H * HD) ** -0.5, 0.046875, ((0, 4), (1, 32)))
    norm_gain = jnp.clip(1.0 + 0.18 * jax.random.normal(key_of[7], (D,), jnp.float32), 0.099609375, 1.8984375).astype(jnp.bfloat16)
    gate_weight = centred(key_of[8], (D, FF_WIN), D ** -0.5, 0.046875, ((1, 128),))
    up_weight = centred(key_of[9], (D, FF_WIN), D ** -0.5, 0.046875, ((1, 128),))
    return dict(queries=queries, kv_cache=kv_cache, new_kv=new_kv, offsets=offsets, lengths=lengths, residual=residual, out_weight=out_weight, norm_gain=norm_gain, gate_weight=gate_weight, up_weight=up_weight)


def reference(queries, kv_cache, new_kv, offsets, lengths, residual, out_weight, norm_gain, gate_weight, up_weight):
    group = H // KVH
    inv_root = 1.0 / HD ** 0.5
    query_heads = queries.astype(jnp.float32).reshape(ROWS, KVH, group, HD)
    cache_keys = kv_cache[:, :, 0, :].astype(jnp.float32).reshape(ROWS, SEQ, KVH, HD)
    cache_values = kv_cache[:, :, 1, :].astype(jnp.float32).reshape(ROWS, SEQ, KVH, HD)
    scores = jnp.einsum('bgqd,bsgd->bgqs', query_heads, cache_keys) * inv_root
    slot_ids = jnp.arange(SEQ, dtype=jnp.int32)
    shard_ids = slot_ids // S_DEV
    positions = (shard_ids[None, :] - offsets[:, None]) % KV_SHARDS * S_DEV + (slot_ids % S_DEV)[None, :]
    live_slots = positions < lengths[:, None]
    scores = jnp.where(live_slots[:, None, None, :], scores, -jnp.inf)
    new_keys = new_kv[:, 0, :].astype(jnp.float32).reshape(ROWS, KVH, HD)
    new_values = new_kv[:, 1, :].astype(jnp.float32).reshape(ROWS, KVH, HD)
    score_new = jnp.einsum('bgqd,bgd->bgq', query_heads, new_keys) * inv_root
    top_score = jnp.maximum(lax.optimization_barrier(jnp.max(scores, axis=-1)), score_new)
    weight_old = jnp.exp(scores - top_score[..., None])
    weight_new = jnp.exp(score_new - top_score)
    total_weight = lax.optimization_barrier(jnp.sum(weight_old, axis=-1)) + weight_new
    rounded_old = weight_old.astype(jnp.bfloat16).astype(jnp.float32)
    rounded_new = weight_new.astype(jnp.bfloat16).astype(jnp.float32)
    summed = jnp.einsum('bgqs,bsgd->bgqd', rounded_old, cache_values)
    summed = summed + rounded_new[..., None] * new_values[:, :, None, :]
    attn = (summed / total_weight[..., None]).astype(jnp.bfloat16).reshape(ROWS, H * HD)
    projected = jnp.dot(attn, out_weight, preferred_element_type=jnp.float32)
    stream = (residual.astype(jnp.float32) + projected).astype(jnp.bfloat16)
    stream_wide = stream.astype(jnp.float32)
    mean_square = lax.optimization_barrier(jnp.sum(stream_wide * stream_wide, axis=1)) / D
    normed = (stream_wide * jax.lax.rsqrt(mean_square + 1e-05)[:, None] * norm_gain.astype(jnp.float32)[None, :]).astype(jnp.bfloat16)
    gate = jnp.dot(normed, gate_weight, preferred_element_type=jnp.float32)
    up_part = jnp.dot(normed, up_weight, preferred_element_type=jnp.float32)
    gated = (jax.nn.silu(gate) * up_part).astype(jnp.bfloat16)
    return (stream, gated)
```

```python
import jax
import jax.numpy as jnp
from jax import lax
from jax.experimental import pallas as pl
from jax.experimental.pallas import tpu as pltpu
from jax.sharding import PartitionSpec as P

D = 16384
HD = 128
F32 = jnp.float32
BF16 = jnp.bfloat16
VMEM = pl.BlockSpec(memory_space=pltpu.VMEM)
SMEM = pl.BlockSpec(memory_space=pltpu.SMEM)
ANY = pl.BlockSpec(memory_space=pl.ANY)
MIB = 1 << 20


def attention_kernel(offs, lens, q_ref, new_ref, cache, out_ref, buf, q_by_row, values, stats, sems):
    rows, width, _ = cache.shape
    heads = q_ref.shape[1] // HD
    group = heads // 2
    slots = width // 4
    copies = [pltpu.make_async_copy(cache.at[b], buf.at[b], sems.at[b]) for b in range(rows)]
    for copy in copies:
        copy.start()
    place = lax.axis_index("kv")
    shards = lax.axis_size("kv")
    for h in range(heads):
        q_by_row[pl.ds(h, rows, heads), :] = q_ref[:, h * HD : (h + 1) * HD].astype(F32)
    inv_root = 1.0 / HD**0.5
    column = lax.broadcasted_iota(jnp.int32, (heads, width), 1)
    row = lax.broadcasted_iota(jnp.int32, (heads, width), 0)
    is_key = (column & 3) == jnp.where(row >= group, 2, 0)
    lane = lax.broadcasted_iota(jnp.int32, (heads, HD), 1)
    second = lax.broadcasted_iota(jnp.int32, (heads, HD), 0) >= group
    for b in range(rows):
        copies[b].wait()
        shard = lax.rem(place - offs[b] + shards, shards)
        limit = (lens[b] - shard * slots) * 4
        q = q_by_row[b * heads : (b + 1) * heads, :]
        x = buf[b]
        raw = lax.dot_general(
            q.astype(BF16), x, (((1,), (1,)), ((), ())), preferred_element_type=F32
        )
        scores = jnp.where(is_key & (column < limit), raw * inv_root, -jnp.inf)
        new = new_ref[b].astype(F32)
        key_new = jnp.where(second, new[0:1, HD:], new[0:1, :HD])
        value_new = jnp.where(second, new[1:2, HD:], new[1:2, :HD])
        score_new = jnp.sum(q * key_new, axis=1, keepdims=True) * inv_root
        score_new = jnp.where(place == 0, score_new, -jnp.inf)
        top = jnp.maximum(jnp.maximum(jnp.max(scores, axis=1, keepdims=True), score_new), -1e30)
        top = top.astype(BF16).astype(F32)
        weight = jnp.exp(scores - top)
        weight_new = jnp.exp(score_new - top)
        total = jnp.sum(weight, axis=1, keepdims=True) + weight_new
        moved = jnp.concatenate(
            [pltpu.roll(weight[:, c : c + HD], 1, 1) for c in range(0, width, HD)], axis=1
        ).astype(BF16)
        summed = jnp.dot(moved, x, preferred_element_type=F32)
        summed = summed + weight_new.astype(BF16).astype(F32) * value_new
        values[pl.ds(b, heads, rows), :] = summed
        stats[pl.ds(b, heads, rows), :] = jnp.where(lane < HD // 2, top, total)
    both = jnp.concatenate(
        [values[...].reshape(heads, rows, HD), stats[...].reshape(heads, rows, HD)], axis=1
    )
    out_ref[...] = both.astype(BF16)


def combine_kernel(parts_ref, out_ref):
    parts = parts_ref[...].astype(F32)
    rows = parts.shape[1] // 2
    value, stat = parts[:, :rows], parts[:, rows:]
    top, total = stat[:, :, 0:1], stat[:, :, HD // 2 : HD // 2 + 1]
    factor = jnp.exp(top - jnp.max(top, axis=0, keepdims=True))
    joint = jnp.sum(value * factor, axis=0) / jnp.sum(total * factor, axis=0)
    out_ref[...] = jnp.broadcast_to(joint.astype(BF16)[None], out_ref.shape)


def project_kernel(attn_ref, residual_ref, gain_ref, weight, out_ref, buf, sems):
    chunks = buf.shape[0]
    depth = weight.shape[0] // chunks
    width = weight.shape[1]
    copies = [
        pltpu.make_async_copy(weight.at[pl.ds(c * depth, depth)], buf.at[c], sems.at[c])
        for c in range(chunks)
    ]
    for copy in copies:
        copy.start()
    heads = depth // HD
    total = None
    for c in range(chunks):
        lhs = jnp.concatenate([attn_ref[c * heads + h] for h in range(heads)], axis=1)
        copies[c].wait()
        part = jnp.dot(lhs, buf[c], preferred_element_type=F32)
        total = part if total is None else total + part
    rows = total.shape[0]
    mine = lax.broadcasted_iota(jnp.int32, (rows, width), 1) // HD == lax.axis_index("head")
    residual = jnp.concatenate([residual_ref[...].astype(F32)] * (width // HD), axis=1)
    total = total + jnp.where(mine, residual, 0.0)
    gain = jnp.broadcast_to(gain_ref[...].astype(F32).reshape(1, HD), (rows, HD))
    block = jnp.concatenate([total, gain], axis=1)
    out_ref[...] = jnp.broadcast_to(block[None], out_ref.shape)


def stream_kernel(parts_ref, stream_ref, out_ref):
    parts = parts_ref[...]
    heads, rows, width = parts.shape
    width -= HD
    total = parts[0, :, :width]
    for h in range(1, heads):
        total = total + parts[h, :, :width]
    stream = total.astype(BF16)
    wide = stream.astype(F32)
    gain = jnp.concatenate([parts[h, :, width:] for h in range(heads)], axis=1)
    squares = jnp.sum(wide * wide, axis=1, keepdims=True)
    high = squares.astype(BF16).astype(F32)
    lane = lax.broadcasted_iota(jnp.int32, (rows, HD), 1)
    tail = jnp.where(lane < HD // 2, high, squares - high)
    block = jnp.concatenate([wide * gain, tail], axis=1).astype(BF16)
    out_ref[...] = jnp.broadcast_to(block[None], out_ref.shape)
    head = lax.axis_index("head")
    own = wide[:, :HD]
    for h in range(1, heads):
        own = jnp.where(head == h, wide[:, h * HD : (h + 1) * HD], own)
    stream_ref[...] = own.astype(BF16)


def gated_kernel(x_ref, gate_weight, up_weight, out_ref, gate_buf, up_buf, sems):
    chunks, depth, _ = gate_buf.shape
    copies = []
    for c in range(chunks):
        rows = pl.ds(c * depth, depth)
        copies.append(
            (
                pltpu.make_async_copy(gate_weight.at[rows], gate_buf.at[c], sems.at[0, c]),
                pltpu.make_async_copy(up_weight.at[rows], up_buf.at[c], sems.at[1, c]),
            )
        )
    for pair in copies:
        for copy in pair:
            copy.start()
    width = x_ref.shape[2] - HD
    per_chunk = depth // width
    tail = x_ref[:, :, width:].astype(F32)
    squares = jnp.sum(tail[:, :, 0:1] + tail[:, :, HD // 2 : HD // 2 + 1], axis=0)
    inv_norm = lax.rsqrt(squares / D + 1e-05)
    gate = up = None
    for c in range(chunks):
        lhs = jnp.concatenate([x_ref[c * per_chunk + i, :, :width] for i in range(per_chunk)], axis=1)
        for copy in copies[c]:
            copy.wait()
        gate_part = jnp.dot(lhs, gate_buf[c], preferred_element_type=F32)
        up_part = jnp.dot(lhs, up_buf[c], preferred_element_type=F32)
        gate = gate_part if gate is None else gate + gate_part
        up = up_part if up is None else up + up_part
    gate = gate * inv_norm
    up = up * inv_norm
    out_ref[...] = (gate / (1.0 + jnp.exp(-gate)) * up).astype(BF16)


def params(mib):
    return pltpu.CompilerParams(vmem_limit_bytes=mib * MIB)


def shards(
    queries,
    kv_cache,
    new_kv,
    offsets,
    lengths,
    residual,
    out_weight,
    norm_gain,
    gate_weight,
    up_weight,
):
    rows, slots = kv_cache.shape[:2]
    heads = queries.shape[1] // HD
    kv, head = lax.axis_size("kv"), lax.axis_size("head")
    width = out_weight.shape[1]
    cache = (
        kv_cache.reshape(rows, slots, 2, 2, HD)
        .transpose(0, 1, 3, 2, 4)
        .reshape(rows, slots * 4, HD)
    )
    parts = pl.pallas_call(
        attention_kernel,
        out_shape=jax.ShapeDtypeStruct((heads, 2 * rows, HD), BF16),
        in_specs=[SMEM, SMEM, VMEM, VMEM, ANY],
        out_specs=VMEM,
        scratch_shapes=[
            pltpu.VMEM((rows, slots * 4, HD), BF16),
            pltpu.VMEM((rows * heads, HD), F32),
            pltpu.VMEM((rows * heads, HD), F32),
            pltpu.VMEM((rows * heads, HD), F32),
            pltpu.SemaphoreType.DMA((rows,)),
        ],
        compiler_params=params(16),
        name="attention",
    )(offsets, lengths, queries, new_kv, cache)
    parts = lax.all_to_all(parts, "kv", 0, 0, tiled=True)
    attn = pl.pallas_call(
        combine_kernel,
        out_shape=jax.ShapeDtypeStruct((kv, rows, HD), BF16),
        in_specs=[VMEM],
        out_specs=VMEM,
        compiler_params=params(8),
        name="combine",
    )(parts)
    attn = lax.all_to_all(attn, "kv", 0, 0, tiled=True)
    chunks = 4
    partial = pl.pallas_call(
        project_kernel,
        out_shape=jax.ShapeDtypeStruct((head, rows, width + HD), F32),
        in_specs=[VMEM, VMEM, VMEM, ANY],
        out_specs=VMEM,
        scratch_shapes=[
            pltpu.VMEM((chunks, out_weight.shape[0] // chunks, width), BF16),
            pltpu.SemaphoreType.DMA((chunks,)),
        ],
        compiler_params=params(16),
        name="project",
    )(attn, residual, norm_gain, out_weight)
    partial = lax.all_to_all(partial, "head", 0, 0, tiled=True)
    stream, features = pl.pallas_call(
        stream_kernel,
        out_shape=(
            jax.ShapeDtypeStruct((rows, HD), BF16),
            jax.ShapeDtypeStruct((kv, rows, width + HD), BF16),
        ),
        in_specs=[VMEM],
        out_specs=(VMEM, VMEM),
        compiler_params=params(8),
        name="stream",
    )(partial)
    features = lax.all_to_all(features, "kv", 0, 0, tiled=True)
    chunks = 8
    columns = gate_weight.shape[1]
    gated = pl.pallas_call(
        gated_kernel,
        out_shape=jax.ShapeDtypeStruct((rows, columns), BF16),
        in_specs=[VMEM, ANY, ANY],
        out_specs=VMEM,
        scratch_shapes=[
            pltpu.VMEM((chunks, D // chunks, columns), BF16),
            pltpu.VMEM((chunks, D // chunks, columns), BF16),
            pltpu.SemaphoreType.DMA((2, chunks)),
        ],
        compiler_params=params(24),
        name="gated",
    )(features, gate_weight, up_weight)
    return (stream, gated)


def solution(mesh):
    in_specs = (
        P(None, "head"),
        P(None, "kv", None, "head"),
        P(None, None, "head"),
        P(),
        P(),
        P(None, ("kv", "head")),
        P("head", "kv"),
        P(("kv", "head")),
        P(None, ("kv", "head")),
        P(None, ("kv", "head")),
    )
    out_specs = (P(None, ("kv", "head")), P(None, ("kv", "head")))
    return jax.shard_map(shards, mesh=mesh, in_specs=in_specs, out_specs=out_specs, check_vma=False)
```

```python
import jax
import jax.numpy as jnp
from jax import lax
from jax.experimental import pallas as pl
from jax.experimental.pallas import tpu as pltpu
from jax.sharding import Mesh
from jax.sharding import PartitionSpec as P

D = 16384
HD = 128
HALF = HD // 2
F32 = jnp.float32
BF16 = jnp.bfloat16
LOG2E = 1.4426950408889634
VMEM = pl.BlockSpec(memory_space=pltpu.VMEM)
HBM = pl.BlockSpec(memory_space=pltpu.HBM)
MIB = 1 << 20
KV = ("y", "x", "core")
ALL = ("y", "x", "core", "head")


def lanes(rows):
    return lax.broadcasted_iota(jnp.int32, (rows, HD), 1)


def attention_kernel(
    offs_hbm, lens_hbm, q_hbm, new_hbm, cache, out_ref, offs, lens, q_ref, new_ref, buf, q_by_row, sems
):
    rows, width, _ = cache.shape
    heads = q_ref.shape[1] // HD
    group = heads // 2
    slots = width // 4
    small = [
        pltpu.make_async_copy(source, target, sems.at[rows + i])
        for i, (source, target) in enumerate(
            ((q_hbm, q_ref), (new_hbm, new_ref), (offs_hbm, offs), (lens_hbm, lens))
        )
    ]
    copies = [pltpu.make_async_copy(cache.at[b], buf.at[b], sems.at[b]) for b in range(rows)]
    for copy in small + copies:
        copy.start()
    place = (lax.axis_index("y") * lax.axis_size("x") + lax.axis_index("x")) * lax.axis_size(
        "core"
    ) + lax.axis_index("core")
    shards = lax.axis_size("y") * lax.axis_size("x") * lax.axis_size("core")
    inv_root = 1.0 / HD**0.5
    lane = lanes(2 * group)
    first = (lane & 2) == 0
    low = lax.broadcasted_iota(jnp.int32, (2 * group, 1), 0) < group
    stat_lane = lanes(group)
    stats = [jnp.zeros((group, HD), F32), jnp.zeros((group, HD), F32)]
    for copy in small:
        copy.wait()
    for h in range(heads):
        q_by_row[pl.ds(h, rows, heads), :] = q_ref[:, h * HD : (h + 1) * HD].astype(F32)
    for b in range(0, rows, 2):
        limits, new_scores, new_values, queries = [], [], [], []
        for i in (b, b + 1):
            shard = lax.rem(place - offs[i] + shards, shards)
            limits.append((lens[i] - shard * slots) * 4)
            q = q_by_row[i * heads : (i + 1) * heads, :]
            new = new_ref[i].astype(F32)
            key_new = jnp.where(low, new[0:1, :HD], new[0:1, HD:])
            new_values.append(jnp.where(low, new[1:2, :HD], new[1:2, HD:]))
            score_new = jnp.sum(q * key_new, axis=1, keepdims=True) * inv_root
            new_scores.append(jnp.where(place == 0, score_new, -jnp.inf))
            queries.append(q)
        zero = jnp.zeros((heads, HD), F32)
        q = jnp.concatenate(
            [
                jnp.concatenate([queries[0], zero], axis=1),
                jnp.concatenate([zero, queries[1]], axis=1),
            ],
            axis=0,
        ).astype(BF16)
        copies[b].wait()
        copies[b + 1].wait()
        x = jnp.concatenate([buf[b], buf[b + 1]], axis=1)
        raw = lax.dot_general(q, x, (((1,), (1,)), ((), ())), preferred_element_type=F32)
        left = jnp.where(low, limits[0], limits[1]) - lane
        left = jnp.where((lane & 1) == 0, left, -(1 << 30))
        scores = []
        for c in range(0, width, HD):
            part = raw[:, c : c + HD]
            head0 = jnp.concatenate([part[:group], part[heads : heads + group]], axis=0)
            head1 = jnp.concatenate([part[group:heads], part[heads + group :]], axis=0)
            scores.append(jnp.where(left > c, jnp.where(first, head0, head1), -jnp.inf))
        most = scores[0]
        for part in scores[1:]:
            most = jnp.maximum(most, part)
        tops = []
        for h, mine in enumerate((first, ~first)):
            top = jnp.max(jnp.where(mine, most, -jnp.inf), axis=1, keepdims=True) * inv_root
            new = jnp.concatenate([s[h * group : (h + 1) * group] for s in new_scores], axis=0)
            top = jnp.maximum(jnp.maximum(top, new), -1e30)
            tops.append(top.astype(BF16).astype(F32))
        shift = jnp.where(first, tops[0], tops[1]) * LOG2E
        total = jnp.zeros((2 * group, HD), F32)
        moved = []
        for part in scores:
            weight = jnp.exp2(part * (inv_root * LOG2E) - shift)
            total = total + weight
            moved.append(pltpu.roll(weight, 1, 1))
        moved = [[jnp.where(first, w, 0.0).astype(BF16), jnp.where(first, 0.0, w).astype(BF16)] for w in moved]
        lhs = [
            jnp.concatenate([pair[h][i * group : (i + 1) * group] for pair in moved], axis=1)
            for i in (0, 1)
            for h in (0, 1)
        ]
        summed = jnp.dot(jnp.concatenate(lhs, axis=0), x, preferred_element_type=F32)
        totals = [
            jnp.sum(jnp.where(mine, total, 0.0), axis=1, keepdims=True) for mine in (first, ~first)
        ]
        for i in (0, 1):
            for h in (0, 1):
                mine = slice(i * group, (i + 1) * group)
                theirs = slice(h * group, (h + 1) * group)
                top = tops[h][mine]
                weight_new = jnp.exp(new_scores[i][theirs] - top)
                value = summed[i * heads + h * group :][:group, i * HD : (i + 1) * HD]
                value = value + weight_new.astype(BF16).astype(F32) * new_values[i][theirs]
                block = value.astype(BF16)
                for dest in range(h, out_ref.shape[0], 2):
                    out_ref[dest, (b + i) * group : (b + i + 1) * group, :] = block
                stat = jnp.where(stat_lane == b + i, top, stats[h])
                stats[h] = jnp.where(stat_lane == HALF + b + i, totals[h][mine] + weight_new, stat)
    for h in (0, 1):
        for dest in range(h, out_ref.shape[0], 2):
            out_ref[dest, rows * group :, :] = stats[h].astype(BF16)


def join(parts, rows):
    group = parts[0].shape[0] // (rows + 1)
    stats = [part[rows * group :].astype(F32) for part in parts]
    top = stats[0]
    for stat in stats[1:]:
        top = jnp.maximum(top, stat)
    factors = [jnp.exp(stat - top) for stat in stats]
    total = sum(f * pltpu.roll(stat, HALF, 1) for f, stat in zip(factors, stats))
    sums = []
    for b in range(rows):
        mine = slice(b * group, (b + 1) * group)
        sums.append(sum(part[mine].astype(F32) * f[:, b : b + 1] for part, f in zip(parts, factors)))
    return sums, top, total


def combine_kernel(parts_ref, out_ref):
    parts = [parts_ref[i] for i in range(parts_ref.shape[0])]
    group = 16
    rows = parts_ref.shape[1] // group - 1
    sums, top, total = join(parts, rows)
    stats = jnp.where(lanes(group) < HALF, top, pltpu.roll(total, HALF, 1))
    block = jnp.concatenate(sums + [stats], axis=0).astype(BF16)
    out_ref[...] = jnp.broadcast_to(block[None], out_ref.shape)


def project_kernel(parts_ref, residual_ref, gain_ref, weight_ref, out_ref, attn):
    group = 16
    rows = parts_ref.shape[1] // group - 1
    for h in (0, 1):
        parts = [parts_ref[i] for i in range(h, parts_ref.shape[0], 2)]
        sums, _, total = join(parts, rows)
        for b in range(rows):
            attn[h, b * group : (b + 1) * group, :] = sums[b] / total[:, b : b + 1]
    lhs = jnp.concatenate(
        [attn[h, pl.ds(g, rows, group), :] for h in (0, 1) for g in range(group)], axis=1
    )
    total = jnp.dot(lhs.astype(BF16), weight_ref[...], preferred_element_type=F32)
    gain = jnp.broadcast_to(gain_ref[...].astype(F32).reshape(1, HD), (rows, HD))
    block = jnp.concatenate([total, residual_ref[...].astype(F32), gain], axis=1).astype(BF16)
    out_ref[...] = jnp.broadcast_to(block[None], out_ref.shape)


def stream_kernel(parts_ref, stream_ref, out_ref):
    count, rows, width = parts_ref.shape
    width -= 2 * HD
    heads = width // HD
    parts = parts_ref[...].astype(F32)
    streams, gains = [], []
    for c in range(count // heads):
        mine = [parts[c * heads + h] for h in range(heads)]
        total = sum(part[:, :width] for part in mine)
        streams.append(total + jnp.concatenate([p[:, width : width + HD] for p in mine], axis=1))
        gains.append(jnp.concatenate([p[:, width + HD :] for p in mine], axis=1))
    wide = jnp.concatenate(streams, axis=1).astype(BF16).astype(F32)
    gain = jnp.concatenate(gains, axis=1)
    squares = jnp.sum(wide * wide, axis=1, keepdims=True)
    high = squares.astype(BF16).astype(F32)
    tail = jnp.where(lanes(rows) < HALF, high, squares - high)
    block = jnp.concatenate([wide * gain, tail], axis=1).astype(BF16)
    out_ref[...] = jnp.broadcast_to(block[None], out_ref.shape)
    place = lax.axis_index("core") * lax.axis_size("head") + lax.axis_index("head")
    own = wide[:, :HD]
    for i in range(1, count):
        own = jnp.where(place == i, wide[:, i * HD : (i + 1) * HD], own)
    stream_ref[...] = own.astype(BF16)


def gated_kernel(x_ref, gate_ref, up_ref, out_ref):
    width = x_ref.shape[2] - HD
    tail = x_ref[:, :, width:].astype(F32)
    squares = jnp.sum(tail[:, :, 0:1] + tail[:, :, HALF : HALF + 1], axis=0)
    inv_norm = lax.rsqrt(squares / D + 1e-05)
    lhs = jnp.concatenate([x_ref[i, :, :width] for i in range(x_ref.shape[0])], axis=1)
    gate = jnp.dot(lhs, gate_ref[...], preferred_element_type=F32) * inv_norm
    up = jnp.dot(lhs, up_ref[...], preferred_element_type=F32) * inv_norm
    out_ref[...] = (gate / (1.0 + jnp.exp(-gate)) * up).astype(BF16)


def params(mib):
    return pltpu.CompilerParams(vmem_limit_bytes=mib * MIB)


def kernel_and_exchange():
    return pl.CostEstimate(flops=10**12, bytes_accessed=10**8, transcendentals=0)


def shards(
    queries,
    kv_cache,
    new_kv,
    offsets,
    lengths,
    residual,
    out_weight,
    norm_gain,
    gate_weight,
    up_weight,
):
    rows, slots = kv_cache.shape[:2]
    heads = queries.shape[1] // HD
    group = heads // 2
    ny, nx, nc, nz = (lax.axis_size(name) for name in ALL)
    width = out_weight.shape[1]
    message = rows * group + group
    cache = (
        kv_cache.reshape(rows, slots, 2, 2, HD)
        .transpose(0, 1, 3, 2, 4)
        .reshape(rows, slots * 4, HD)
    )
    parts = pl.pallas_call(
        attention_kernel,
        out_shape=jax.ShapeDtypeStruct((nx * nc, message, HD), BF16),
        in_specs=[HBM] * 5,
        out_specs=VMEM,
        scratch_shapes=[
            pltpu.SMEM(offsets.shape, jnp.int32),
            pltpu.SMEM(lengths.shape, jnp.int32),
            pltpu.VMEM(queries.shape, BF16),
            pltpu.VMEM(new_kv.shape, BF16),
            pltpu.VMEM(cache.shape, BF16),
            pltpu.VMEM((rows * heads, HD), F32),
            pltpu.SemaphoreType.DMA((rows + 4,)),
        ],
        compiler_params=params(60),
        name="attention",
    )(offsets, lengths, queries, new_kv, cache)
    parts = lax.all_to_all(parts, ("x", "core"), 0, 0, tiled=True)
    parts = pl.pallas_call(
        combine_kernel,
        out_shape=jax.ShapeDtypeStruct((ny * nc, message, HD), BF16),
        in_specs=[VMEM],
        out_specs=VMEM,
        compiler_params=params(8),
        cost_estimate=kernel_and_exchange(),
        name="combine",
    )(parts)
    parts = lax.all_to_all(parts, ("y", "core"), 0, 0, tiled=True)
    partial = pl.pallas_call(
        project_kernel,
        out_shape=jax.ShapeDtypeStruct((nc * nz, rows, width + 2 * HD), BF16),
        in_specs=[VMEM] * 4,
        out_specs=VMEM,
        scratch_shapes=[pltpu.VMEM((2, rows * group, HD), F32)],
        compiler_params=params(8),
        name="project",
    )(parts, residual, norm_gain, out_weight)
    partial = lax.all_to_all(partial, ("core", "head"), 0, 0, tiled=True)
    stream, features = pl.pallas_call(
        stream_kernel,
        out_shape=(
            jax.ShapeDtypeStruct((rows, HD), BF16),
            jax.ShapeDtypeStruct((ny * nx, rows, nc * width + HD), BF16),
        ),
        in_specs=[VMEM],
        out_specs=(VMEM, VMEM),
        compiler_params=params(8),
        cost_estimate=kernel_and_exchange(),
        name="stream",
    )(partial)
    features = lax.all_to_all(features, ("y", "x"), 0, 0, tiled=True)
    gated = pl.pallas_call(
        gated_kernel,
        out_shape=jax.ShapeDtypeStruct((rows, gate_weight.shape[1]), BF16),
        in_specs=[VMEM] * 3,
        out_specs=VMEM,
        compiler_params=params(24),
        name="gated",
    )(features, gate_weight, up_weight)
    return (stream, gated)


def solution(mesh):
    split = Mesh(mesh.devices.reshape(4, 4, 2, 4), ALL)
    in_specs = (
        P(None, "head"),
        P(None, KV, None, "head"),
        P(None, None, "head"),
        P(),
        P(),
        P(None, ALL),
        P("head", KV),
        P(ALL),
        P(None, ALL),
        P(None, ALL),
    )
    out_specs = (P(None, ALL), P(None, ALL))
    return jax.shard_map(shards, mesh=split, in_specs=in_specs, out_specs=out_specs, check_vma=False)
```

```python
import jax
import jax.numpy as jnp
from jax import lax
from jax.experimental import pallas as pl
from jax.experimental.pallas import tpu as pltpu
from jax.sharding import Mesh
from jax.sharding import PartitionSpec as P

D = 16384
HD = 128
HALF = HD // 2
F32 = jnp.float32
BF16 = jnp.bfloat16
LOG2E = 1.4426950408889634
VMEM = pl.BlockSpec(memory_space=pltpu.VMEM)
HBM = pl.BlockSpec(memory_space=pltpu.HBM)
MIB = 1 << 20
KV = ("y", "x", "core")
ALL = ("y", "x", "core", "head")


def lanes(rows):
    return lax.broadcasted_iota(jnp.int32, (rows, HD), 1)


def attention_kernel(
    offs_hbm, lens_hbm, q_hbm, new_hbm, cache, out_ref, offs, lens, q_ref, new_ref, buf, q_by_row, sems
):
    rows, width, _ = cache.shape
    heads = q_ref.shape[1] // HD
    group = heads // 2
    slots = width // 4
    small = [
        pltpu.make_async_copy(source, target, sems.at[rows + i])
        for i, (source, target) in enumerate(
            ((q_hbm, q_ref), (new_hbm, new_ref), (offs_hbm, offs), (lens_hbm, lens))
        )
    ]
    copies = [pltpu.make_async_copy(cache.at[b], buf.at[b], sems.at[b]) for b in range(rows)]
    for copy in small + copies:
        copy.start()
    place = (lax.axis_index("y") * lax.axis_size("x") + lax.axis_index("x")) * lax.axis_size(
        "core"
    ) + lax.axis_index("core")
    shards = lax.axis_size("y") * lax.axis_size("x") * lax.axis_size("core")
    inv_root = 1.0 / HD**0.5
    lane = lanes(2 * group)
    first = (lane & 2) == 0
    low = lax.broadcasted_iota(jnp.int32, (2 * group, 1), 0) < group
    stat_lane = lanes(group)
    stats = [jnp.zeros((group, HD), F32), jnp.zeros((group, HD), F32)]
    for copy in small:
        copy.wait()
    for h in range(heads):
        q_by_row[pl.ds(h, rows, heads), :] = q_ref[:, h * HD : (h + 1) * HD].astype(F32)
    def products(b):
        limits, new_scores, new_values, queries = [], [], [], []
        for i in (b, b + 1):
            shard = lax.rem(place - offs[i] + shards, shards)
            limits.append((lens[i] - shard * slots) * 4)
            q = q_by_row[i * heads : (i + 1) * heads, :]
            new = new_ref[i].astype(F32)
            key_new = jnp.where(low, new[0:1, :HD], new[0:1, HD:])
            new_values.append(jnp.where(low, new[1:2, :HD], new[1:2, HD:]))
            score_new = jnp.sum(q * key_new, axis=1, keepdims=True) * inv_root
            new_scores.append(jnp.where(place == 0, score_new, -jnp.inf))
            queries.append(q)
        zero = jnp.zeros((heads, HD), F32)
        q = jnp.concatenate(
            [
                jnp.concatenate([queries[0], zero], axis=1),
                jnp.concatenate([zero, queries[1]], axis=1),
            ],
            axis=0,
        ).astype(BF16)
        copies[b].wait()
        copies[b + 1].wait()
        x = jnp.concatenate([buf[b], buf[b + 1]], axis=1)
        raw = lax.dot_general(q, x, (((1,), (1,)), ((), ())), preferred_element_type=F32)
        return x, raw, limits, new_scores, new_values

    ahead = products(0)
    for b in range(0, rows, 2):
        x, raw, limits, new_scores, new_values = ahead
        if b + 2 < rows:
            ahead = products(b + 2)
        left = jnp.where(low, limits[0], limits[1]) - lane
        left = jnp.where((lane & 1) == 0, left, -(1 << 30))
        scores = []
        for c in range(0, width, HD):
            part = raw[:, c : c + HD]
            head0 = jnp.concatenate([part[:group], part[heads : heads + group]], axis=0)
            head1 = jnp.concatenate([part[group:heads], part[heads + group :]], axis=0)
            scores.append(jnp.where(left > c, jnp.where(first, head0, head1), -jnp.inf))
        most = scores[0]
        for part in scores[1:]:
            most = jnp.maximum(most, part)
        tops = []
        for h, mine in enumerate((first, ~first)):
            top = jnp.max(jnp.where(mine, most, -jnp.inf), axis=1, keepdims=True) * inv_root
            new = jnp.concatenate([s[h * group : (h + 1) * group] for s in new_scores], axis=0)
            top = jnp.maximum(jnp.maximum(top, new), -1e30)
            tops.append(top.astype(BF16).astype(F32))
        shift = jnp.where(first, tops[0], tops[1]) * LOG2E
        total = jnp.zeros((2 * group, HD), F32)
        moved = []
        for part in scores:
            weight = jnp.exp2(part * (inv_root * LOG2E) - shift)
            total = total + weight
            moved.append(pltpu.roll(weight, 1, 1))
        moved = [[jnp.where(first, w, 0.0).astype(BF16), jnp.where(first, 0.0, w).astype(BF16)] for w in moved]
        lhs = [
            jnp.concatenate([pair[h][i * group : (i + 1) * group] for pair in moved], axis=1)
            for i in (0, 1)
            for h in (0, 1)
        ]
        summed = jnp.dot(jnp.concatenate(lhs, axis=0), x, preferred_element_type=F32)
        totals = [
            jnp.sum(jnp.where(mine, total, 0.0), axis=1, keepdims=True) for mine in (first, ~first)
        ]
        for i in (0, 1):
            for h in (0, 1):
                mine = slice(i * group, (i + 1) * group)
                theirs = slice(h * group, (h + 1) * group)
                top = tops[h][mine]
                weight_new = jnp.exp(new_scores[i][theirs] - top)
                value = summed[i * heads + h * group :][:group, i * HD : (i + 1) * HD]
                value = value + weight_new.astype(BF16).astype(F32) * new_values[i][theirs]
                block = value.astype(BF16)
                for dest in range(h, out_ref.shape[0], 2):
                    out_ref[dest, (b + i) * group : (b + i + 1) * group, :] = block
                stat = jnp.where(stat_lane == b + i, top, stats[h])
                stats[h] = jnp.where(stat_lane == HALF + b + i, totals[h][mine] + weight_new, stat)
    for h in (0, 1):
        for dest in range(h, out_ref.shape[0], 2):
            out_ref[dest, rows * group :, :] = stats[h].astype(BF16)


def join(parts, rows):
    group = parts[0].shape[0] // (rows + 1)
    stats = [part[rows * group :].astype(F32) for part in parts]
    top = stats[0]
    for stat in stats[1:]:
        top = jnp.maximum(top, stat)
    factors = [jnp.exp(stat - top) for stat in stats]
    total = sum(f * pltpu.roll(stat, HALF, 1) for f, stat in zip(factors, stats))
    sums = []
    for b in range(rows):
        mine = slice(b * group, (b + 1) * group)
        sums.append(sum(part[mine].astype(F32) * f[:, b : b + 1] for part, f in zip(parts, factors)))
    return sums, top, total


def combine_kernel(parts_ref, out_ref):
    parts = [parts_ref[i] for i in range(parts_ref.shape[0])]
    group = 16
    rows = parts_ref.shape[1] // group - 1
    sums, top, total = join(parts, rows)
    stats = jnp.where(lanes(group) < HALF, top, pltpu.roll(total, HALF, 1))
    block = jnp.concatenate(sums + [stats], axis=0).astype(BF16)
    out_ref[...] = jnp.broadcast_to(block[None], out_ref.shape)


def project_kernel(parts_ref, residual_ref, gain_ref, weight_ref, out_ref, attn):
    group = 16
    rows = parts_ref.shape[1] // group - 1
    for h in (0, 1):
        parts = [parts_ref[i] for i in range(h, parts_ref.shape[0], 2)]
        sums, _, total = join(parts, rows)
        for b in range(rows):
            attn[h, b * group : (b + 1) * group, :] = sums[b] / total[:, b : b + 1]
    lhs = jnp.concatenate(
        [attn[h, pl.ds(g, rows, group), :] for h in (0, 1) for g in range(group)], axis=1
    )
    total = jnp.dot(lhs.astype(BF16), weight_ref[...], preferred_element_type=F32)
    gain = jnp.broadcast_to(gain_ref[...].astype(F32).reshape(1, HD), (rows, HD))
    block = jnp.concatenate([total, residual_ref[...].astype(F32), gain], axis=1).astype(BF16)
    out_ref[...] = jnp.broadcast_to(block[None], out_ref.shape)


def stream_kernel(parts_ref, own_ref, out_ref):
    count, rows, width = parts_ref.shape
    width -= 2 * HD
    heads = width // HD
    parts = parts_ref[...].astype(F32)
    streams, gains = [], []
    for c in range(count // heads):
        mine = [parts[c * heads + h] for h in range(heads)]
        total = sum(part[:, :width] for part in mine)
        streams.append(total + jnp.concatenate([p[:, width : width + HD] for p in mine], axis=1))
        gains.append(jnp.concatenate([p[:, width + HD :] for p in mine], axis=1))
    wide = jnp.concatenate(streams, axis=1).astype(BF16).astype(F32)
    gain = jnp.concatenate(gains, axis=1)
    squares = jnp.sum(wide * wide, axis=1, keepdims=True)
    high = squares.astype(BF16).astype(F32)
    tail = jnp.where(lanes(rows) < HALF, high, squares - high)
    block = jnp.concatenate([wide * gain, tail], axis=1).astype(BF16)
    out_ref[...] = jnp.broadcast_to(block[None], out_ref.shape)
    place = lax.axis_index("core") * lax.axis_size("head") + lax.axis_index("head")
    own = wide[:, :HD]
    for i in range(1, count):
        own = jnp.where(place == i, wide[:, i * HD : (i + 1) * HD], own)
    own_ref[...] = own.astype(BF16)


def gated_kernel(x_ref, own_ref, gate_ref, up_ref, stream_ref, out_ref):
    stream_ref[...] = own_ref[...]
    width = x_ref.shape[2] - HD
    tail = x_ref[:, :, width:].astype(F32)
    squares = jnp.sum(tail[:, :, 0:1] + tail[:, :, HALF : HALF + 1], axis=0)
    inv_norm = lax.rsqrt(squares / D + 1e-05)
    lhs = jnp.concatenate([x_ref[i, :, :width] for i in range(x_ref.shape[0])], axis=1)
    gate = jnp.dot(lhs, gate_ref[...], preferred_element_type=F32) * inv_norm
    up = jnp.dot(lhs, up_ref[...], preferred_element_type=F32) * inv_norm
    out_ref[...] = (gate / (1.0 + jnp.exp(-gate)) * up).astype(BF16)


def params(mib):
    return pltpu.CompilerParams(vmem_limit_bytes=mib * MIB)


def kernel_and_exchange():
    return pl.CostEstimate(flops=10**12, bytes_accessed=10**8, transcendentals=0)


def shards(
    queries,
    kv_cache,
    new_kv,
    offsets,
    lengths,
    residual,
    out_weight,
    norm_gain,
    gate_weight,
    up_weight,
):
    rows, slots = kv_cache.shape[:2]
    heads = queries.shape[1] // HD
    group = heads // 2
    ny, nx, nc, nz = (lax.axis_size(name) for name in ALL)
    width = out_weight.shape[1]
    message = rows * group + group
    cache = (
        kv_cache.reshape(rows, slots, 2, 2, HD)
        .transpose(0, 1, 3, 2, 4)
        .reshape(rows, slots * 4, HD)
    )
    parts = pl.pallas_call(
        attention_kernel,
        out_shape=pltpu.VMEM((nx * nc, message, HD), BF16),
        in_specs=[HBM] * 5,
        out_specs=VMEM,
        scratch_shapes=[
            pltpu.SMEM(offsets.shape, jnp.int32),
            pltpu.SMEM(lengths.shape, jnp.int32),
            pltpu.VMEM(queries.shape, BF16),
            pltpu.VMEM(new_kv.shape, BF16),
            pltpu.VMEM(cache.shape, BF16),
            pltpu.VMEM((rows * heads, HD), F32),
            pltpu.SemaphoreType.DMA((rows + 4,)),
        ],
        compiler_params=params(60),
        name="attention",
    )(offsets, lengths, queries, new_kv, cache)
    parts = lax.all_to_all(parts, ("x", "core"), 0, 0, tiled=True)
    parts = pl.pallas_call(
        combine_kernel,
        out_shape=jax.ShapeDtypeStruct((ny * nc, message, HD), BF16),
        in_specs=[VMEM],
        out_specs=VMEM,
        compiler_params=params(8),
        cost_estimate=kernel_and_exchange(),
        name="combine",
    )(parts)
    parts = lax.all_to_all(parts, ("y", "core"), 0, 0, tiled=True)
    partial = pl.pallas_call(
        project_kernel,
        out_shape=jax.ShapeDtypeStruct((nc * nz, rows, width + 2 * HD), BF16),
        in_specs=[VMEM] * 4,
        out_specs=VMEM,
        scratch_shapes=[pltpu.VMEM((2, rows * group, HD), F32)],
        compiler_params=params(8),
        name="project",
    )(parts, residual, norm_gain, out_weight)
    partial = lax.all_to_all(partial, ("core", "head"), 0, 0, tiled=True)
    own, features = pl.pallas_call(
        stream_kernel,
        out_shape=(
            jax.ShapeDtypeStruct((rows, HD), BF16),
            jax.ShapeDtypeStruct((ny * nx, rows, nc * width + HD), BF16),
        ),
        in_specs=[VMEM],
        out_specs=(VMEM, VMEM),
        compiler_params=params(8),
        cost_estimate=kernel_and_exchange(),
        name="stream",
    )(partial)
    features = lax.all_to_all(features, ("y", "x"), 0, 0, tiled=True)
    return pl.pallas_call(
        gated_kernel,
        out_shape=(
            jax.ShapeDtypeStruct((rows, HD), BF16),
            jax.ShapeDtypeStruct((rows, gate_weight.shape[1]), BF16),
        ),
        in_specs=[VMEM] * 4,
        out_specs=(VMEM, VMEM),
        compiler_params=params(24),
        name="gated",
    )(features, own, gate_weight, up_weight)


def solution(mesh):
    split = Mesh(mesh.devices.reshape(4, 4, 2, 4), ALL)
    in_specs = (
        P(None, "head"),
        P(None, KV, None, "head"),
        P(None, None, "head"),
        P(),
        P(),
        P(None, ALL),
        P("head", KV),
        P(ALL),
        P(None, ALL),
        P(None, ALL),
    )
    out_specs = (P(None, ALL), P(None, ALL))
    return jax.shard_map(shards, mesh=split, in_specs=in_specs, out_specs=out_specs, check_vma=False)
```

```python
import jax
import jax.numpy as jnp
from jax import lax
from jax.experimental import pallas as pl
from jax.experimental.pallas import tpu as pltpu
from jax.sharding import Mesh
from jax.sharding import PartitionSpec as P

D = 16384
HD = 128
HALF = HD // 2
F32 = jnp.float32
BF16 = jnp.bfloat16
LOG2E = 1.4426950408889634
VMEM = pl.BlockSpec(memory_space=pltpu.VMEM)
HBM = pl.BlockSpec(memory_space=pltpu.HBM)
MIB = 1 << 20
KV = ("y", "x", "core")
ALL = ("y", "x", "core", "head")


def lanes(rows):
    return lax.broadcasted_iota(jnp.int32, (rows, HD), 1)


def attention_kernel(
    offs_hbm, lens_hbm, q_hbm, new_hbm, cache, out_ref, offs, lens, q_ref, new_ref, buf, q_by_row, sems
):
    rows, width, _ = cache.shape
    heads = q_ref.shape[1] // HD
    group = heads // 2
    slots = width // 4
    small = [
        pltpu.make_async_copy(source, target, sems.at[rows + i])
        for i, (source, target) in enumerate(
            ((q_hbm, q_ref), (new_hbm, new_ref), (offs_hbm, offs), (lens_hbm, lens))
        )
    ]
    copies = [pltpu.make_async_copy(cache.at[b], buf.at[b], sems.at[b]) for b in range(rows)]
    for copy in small + copies:
        copy.start()
    place = (lax.axis_index("y") * lax.axis_size("x") + lax.axis_index("x")) * lax.axis_size(
        "core"
    ) + lax.axis_index("core")
    shards = lax.axis_size("y") * lax.axis_size("x") * lax.axis_size("core")
    inv_root = 1.0 / HD**0.5
    lane = lanes(2 * group)
    first = (lane & 2) == 0
    low = lax.broadcasted_iota(jnp.int32, (2 * group, 1), 0) < group
    stat_lane = lanes(group)
    stats = [jnp.zeros((group, HD), F32), jnp.zeros((group, HD), F32)]
    for copy in small:
        copy.wait()
    for h in range(heads):
        q_by_row[pl.ds(h, rows, heads), :] = q_ref[:, h * HD : (h + 1) * HD].astype(F32)
    def products(b):
        limits, new_scores, new_values, queries = [], [], [], []
        for i in (b, b + 1):
            shard = lax.rem(place - offs[i] + shards, shards)
            limits.append((lens[i] - shard * slots) * 4)
            q = q_by_row[i * heads : (i + 1) * heads, :]
            new = new_ref[i].astype(F32)
            key_new = jnp.where(low, new[0:1, :HD], new[0:1, HD:])
            new_values.append(jnp.where(low, new[1:2, :HD], new[1:2, HD:]))
            score_new = jnp.sum(q * key_new, axis=1, keepdims=True) * inv_root
            new_scores.append(jnp.where(place == 0, score_new, -jnp.inf))
            queries.append(q)
        zero = jnp.zeros((heads, HD), F32)
        q = jnp.concatenate(
            [
                jnp.concatenate([queries[0], zero], axis=1),
                jnp.concatenate([zero, queries[1]], axis=1),
            ],
            axis=0,
        ).astype(BF16)
        copies[b].wait()
        copies[b + 1].wait()
        x = jnp.concatenate([buf[b], buf[b + 1]], axis=1)
        raw = lax.dot_general(q, x, (((1,), (1,)), ((), ())), preferred_element_type=F32)
        return x, raw, limits, new_scores, new_values

    ahead = products(0)
    for b in range(0, rows, 2):
        x, raw, limits, new_scores, new_values = ahead
        if b + 2 < rows:
            ahead = products(b + 2)
        left = jnp.where(low, limits[0], limits[1]) - lane
        left = jnp.where((lane & 1) == 0, left, -(1 << 30))
        scores = []
        for c in range(0, width, HD):
            part = raw[:, c : c + HD]
            head0 = jnp.concatenate([part[:group], part[heads : heads + group]], axis=0)
            head1 = jnp.concatenate([part[group:heads], part[heads + group :]], axis=0)
            scores.append(jnp.where(left > c, jnp.where(first, head0, head1), -jnp.inf))
        most = scores[0]
        for part in scores[1:]:
            most = jnp.maximum(most, part)
        tops = []
        for h, mine in enumerate((first, ~first)):
            top = jnp.max(jnp.where(mine, most, -jnp.inf), axis=1, keepdims=True) * inv_root
            new = jnp.concatenate([s[h * group : (h + 1) * group] for s in new_scores], axis=0)
            top = jnp.maximum(jnp.maximum(top, new), -1e30)
            tops.append(top.astype(BF16).astype(F32))
        shift = jnp.where(first, tops[0], tops[1]) * LOG2E
        total = jnp.zeros((2 * group, HD), F32)
        moved = []
        for part in scores:
            weight = jnp.exp2(part * (inv_root * LOG2E) - shift)
            total = total + weight
            moved.append(pltpu.roll(weight, 1, 1))
        moved = [[jnp.where(first, w, 0.0).astype(BF16), jnp.where(first, 0.0, w).astype(BF16)] for w in moved]
        lhs = [
            jnp.concatenate([pair[h][i * group : (i + 1) * group] for pair in moved], axis=1)
            for i in (0, 1)
            for h in (0, 1)
        ]
        summed = jnp.dot(jnp.concatenate(lhs, axis=0), x, preferred_element_type=F32)
        totals = [
            jnp.sum(jnp.where(mine, total, 0.0), axis=1, keepdims=True) for mine in (first, ~first)
        ]
        for i in (0, 1):
            for h in (0, 1):
                mine = slice(i * group, (i + 1) * group)
                theirs = slice(h * group, (h + 1) * group)
                top = tops[h][mine]
                weight_new = jnp.exp(new_scores[i][theirs] - top)
                value = summed[i * heads + h * group :][:group, i * HD : (i + 1) * HD]
                value = value + weight_new.astype(BF16).astype(F32) * new_values[i][theirs]
                block = value.astype(BF16)
                for dest in range(h, out_ref.shape[0], 2):
                    out_ref[dest, (b + i) * group : (b + i + 1) * group, :] = block
                stat = jnp.where(stat_lane == b + i, top, stats[h])
                stats[h] = jnp.where(stat_lane == HALF + b + i, totals[h][mine] + weight_new, stat)
    for h in (0, 1):
        for dest in range(h, out_ref.shape[0], 2):
            out_ref[dest, rows * group :, :] = stats[h].astype(BF16)


def join(parts, rows):
    group = parts[0].shape[0] // (rows + 1)
    stats = [part[rows * group :].astype(F32) for part in parts]
    top = stats[0]
    for stat in stats[1:]:
        top = jnp.maximum(top, stat)
    factors = [jnp.exp(stat - top) for stat in stats]
    total = sum(f * pltpu.roll(stat, HALF, 1) for f, stat in zip(factors, stats))
    sums = []
    for b in range(rows):
        mine = slice(b * group, (b + 1) * group)
        sums.append(sum(part[mine].astype(F32) * f[:, b : b + 1] for part, f in zip(parts, factors)))
    return sums, top, total


def combine_kernel(parts_ref, out_ref):
    parts = [parts_ref[i] for i in range(parts_ref.shape[0])]
    group = 16
    rows = parts_ref.shape[1] // group - 1
    sums, top, total = join(parts, rows)
    stats = jnp.where(lanes(group) < HALF, top, pltpu.roll(total, HALF, 1))
    block = jnp.concatenate(sums + [stats], axis=0).astype(BF16)
    out_ref[...] = jnp.broadcast_to(block[None], out_ref.shape)


def project_kernel(parts_ref, residual_ref, gain_ref, own_ref, theirs_ref, out_ref, attn):
    group = 16
    rows = parts_ref.shape[1] // group - 1
    sums, _, total = join([parts_ref[i] for i in range(parts_ref.shape[0])], rows)
    for b in range(rows):
        attn[b * group : (b + 1) * group, :] = sums[b] / total[:, b : b + 1]
    lhs = jnp.concatenate([attn[pl.ds(g, rows, group), :] for g in range(group)], axis=1).astype(BF16)
    mine = pl.ds(pl.multiple_of(lax.axis_index("core") * (group * HD), group * HD), group * HD)
    own = jnp.dot(lhs, own_ref[mine, :], preferred_element_type=F32)
    theirs = jnp.dot(lhs, theirs_ref[mine, :], preferred_element_type=F32)
    core0 = lax.axis_index("core") == 0
    total = jnp.concatenate([jnp.where(core0, own, theirs), jnp.where(core0, theirs, own)], axis=1)
    gain = jnp.broadcast_to(gain_ref[...].astype(F32).reshape(1, HD), (rows, HD))
    block = jnp.concatenate([total, residual_ref[...].astype(F32), gain], axis=1).astype(BF16)
    out_ref[...] = jnp.broadcast_to(block[None], out_ref.shape)


def stream_kernel(parts_ref, own_ref, out_ref):
    count, rows, width = parts_ref.shape
    width -= 2 * HD
    parts = parts_ref[...].astype(F32)
    total = parts[0, :, :width]
    for i in range(1, count):
        total = total + parts[i, :, :width]
    residual = jnp.concatenate([parts[i, :, width : width + HD] for i in range(count)], axis=1)
    wide = (total + residual).astype(BF16).astype(F32)
    gain = jnp.concatenate([parts[i, :, width + HD :] for i in range(count)], axis=1)
    squares = jnp.sum(wide * wide, axis=1, keepdims=True)
    high = squares.astype(BF16).astype(F32)
    tail = jnp.where(lanes(rows) < HALF, high, squares - high)
    block = jnp.concatenate([wide * gain, tail], axis=1).astype(BF16)
    out_ref[...] = jnp.broadcast_to(block[None], out_ref.shape)
    place = lax.axis_index("core") * lax.axis_size("head") + lax.axis_index("head")
    own = wide[:, :HD]
    for i in range(1, count):
        own = jnp.where(place == i, wide[:, i * HD : (i + 1) * HD], own)
    own_ref[...] = own.astype(BF16)


def gated_kernel(x_ref, own_ref, gate_ref, up_ref, stream_ref, out_ref):
    stream_ref[...] = own_ref[...]
    width = x_ref.shape[2] - HD
    tail = x_ref[:, :, width:].astype(F32)
    squares = jnp.sum(tail[:, :, 0:1] + tail[:, :, HALF : HALF + 1], axis=0)
    inv_norm = lax.rsqrt(squares / D + 1e-05)
    lhs = jnp.concatenate([x_ref[i, :, :width] for i in range(x_ref.shape[0])], axis=1)
    gate = jnp.dot(lhs, gate_ref[...], preferred_element_type=F32) * inv_norm
    up = jnp.dot(lhs, up_ref[...], preferred_element_type=F32) * inv_norm
    out_ref[...] = (gate / (1.0 + jnp.exp(-gate)) * up).astype(BF16)


def params(mib):
    return pltpu.CompilerParams(vmem_limit_bytes=mib * MIB)


def kernel_and_exchange():
    return pl.CostEstimate(flops=10**10, bytes_accessed=10**8, transcendentals=0)


def shards(
    queries,
    kv_cache,
    new_kv,
    offsets,
    lengths,
    residual,
    out_weight,
    norm_gain,
    gate_weight,
    up_weight,
):
    rows, slots = kv_cache.shape[:2]
    heads = queries.shape[1] // HD
    group = heads // 2
    ny, nx, nc, nz = (lax.axis_size(name) for name in ALL)
    width = out_weight.shape[1]
    message = rows * group + group
    cache = (
        kv_cache.reshape(rows, slots, 2, 2, HD)
        .transpose(0, 1, 3, 2, 4)
        .reshape(rows, slots * 4, HD)
    )
    parts = pl.pallas_call(
        attention_kernel,
        out_shape=pltpu.VMEM((nx * nc, message, HD), BF16),
        in_specs=[HBM] * 5,
        out_specs=VMEM,
        scratch_shapes=[
            pltpu.SMEM(offsets.shape, jnp.int32),
            pltpu.SMEM(lengths.shape, jnp.int32),
            pltpu.VMEM(queries.shape, BF16),
            pltpu.VMEM(new_kv.shape, BF16),
            pltpu.VMEM(cache.shape, BF16),
            pltpu.VMEM((rows * heads, HD), F32),
            pltpu.SemaphoreType.DMA((rows + 4,)),
        ],
        compiler_params=params(60),
        name="attention",
    )(offsets, lengths, queries, new_kv, cache)
    parts, moving = lax.optimization_barrier((parts, out_weight))
    theirs = lax.ppermute(moving, "core", [(0, 1), (1, 0)])
    parts = lax.all_to_all(parts, ("x", "core"), 0, 0, tiled=True)
    parts, theirs = lax.optimization_barrier((parts, theirs))
    parts = pl.pallas_call(
        combine_kernel,
        out_shape=jax.ShapeDtypeStruct((ny, message, HD), BF16),
        in_specs=[VMEM],
        out_specs=VMEM,
        compiler_params=params(8),
        cost_estimate=kernel_and_exchange(),
        name="combine",
    )(parts)
    parts = lax.all_to_all(parts, "y", 0, 0, tiled=True)
    partial = pl.pallas_call(
        project_kernel,
        out_shape=jax.ShapeDtypeStruct((nc * nz, rows, nc * width + 2 * HD), BF16),
        in_specs=[VMEM] * 5,
        out_specs=VMEM,
        scratch_shapes=[pltpu.VMEM((rows * group, HD), F32)],
        compiler_params=params(12),
        name="project",
    )(parts, residual, norm_gain, out_weight, theirs)
    partial = lax.all_to_all(partial, ("core", "head"), 0, 0, tiled=True)
    own, features = pl.pallas_call(
        stream_kernel,
        out_shape=(
            jax.ShapeDtypeStruct((rows, HD), BF16),
            jax.ShapeDtypeStruct((ny * nx, rows, nc * width + HD), BF16),
        ),
        in_specs=[VMEM],
        out_specs=(VMEM, VMEM),
        compiler_params=params(8),
        cost_estimate=kernel_and_exchange(),
        name="stream",
    )(partial)
    features = lax.all_to_all(features, ("y", "x"), 0, 0, tiled=True)
    return pl.pallas_call(
        gated_kernel,
        out_shape=(
            jax.ShapeDtypeStruct((rows, HD), BF16),
            jax.ShapeDtypeStruct((rows, gate_weight.shape[1]), BF16),
        ),
        in_specs=[VMEM] * 4,
        out_specs=(VMEM, VMEM),
        compiler_params=params(24),
        name="gated",
    )(features, own, gate_weight, up_weight)


def solution(mesh):
    split = Mesh(mesh.devices.reshape(4, 4, 2, 4), ALL)
    in_specs = (
        P(None, "head"),
        P(None, KV, None, "head"),
        P(None, None, "head"),
        P(),
        P(),
        P(None, ALL),
        P("head", KV),
        P(ALL),
        P(None, ALL),
        P(None, ALL),
    )
    out_specs = (P(None, ALL), P(None, ALL))
    return jax.shard_map(shards, mesh=split, in_specs=in_specs, out_specs=out_specs, check_vma=False)
```

```python
import jax
import jax.numpy as jnp
from jax import lax
from jax.experimental import pallas as pl
from jax.experimental.pallas import tpu as pltpu
from jax.sharding import Mesh
from jax.sharding import PartitionSpec as P

D = 16384
HD = 128
HALF = HD // 2
F32 = jnp.float32
BF16 = jnp.bfloat16
LOG2E = 1.4426950408889634
VMEM = pl.BlockSpec(memory_space=pltpu.VMEM)
HBM = pl.BlockSpec(memory_space=pltpu.HBM)
MIB = 1 << 20
KV = ("y", "x", "core")
ALL = ("y", "x", "core", "head")


def lanes(rows):
    return lax.broadcasted_iota(jnp.int32, (rows, HD), 1)


def attention_kernel(
    offs_hbm, lens_hbm, q_hbm, new_hbm, cache, out_ref, offs, lens, q_ref, new_ref, buf, q_by_row, sems
):
    rows, width, _ = cache.shape
    heads = q_ref.shape[1] // HD
    group = heads // 2
    slots = width // 4
    small = [
        pltpu.make_async_copy(source, target, sems.at[rows + i])
        for i, (source, target) in enumerate(
            ((q_hbm, q_ref), (new_hbm, new_ref), (offs_hbm, offs), (lens_hbm, lens))
        )
    ]
    copies = [pltpu.make_async_copy(cache.at[b], buf.at[b], sems.at[b]) for b in range(rows)]
    for copy in small + copies:
        copy.start()
    place = (lax.axis_index("y") * lax.axis_size("x") + lax.axis_index("x")) * lax.axis_size(
        "core"
    ) + lax.axis_index("core")
    shards = lax.axis_size("y") * lax.axis_size("x") * lax.axis_size("core")
    inv_root = 1.0 / HD**0.5
    lane = lanes(2 * group)
    first = (lane & 2) == 0
    low = lax.broadcasted_iota(jnp.int32, (2 * group, 1), 0) < group
    stat_lane = lanes(group)
    stats = [jnp.zeros((group, HD), F32), jnp.zeros((group, HD), F32)]
    for copy in small:
        copy.wait()
    for h in range(heads):
        q_by_row[pl.ds(h, rows, heads), :] = q_ref[:, h * HD : (h + 1) * HD].astype(F32)
    def products(b):
        limits, new_scores, new_values, queries = [], [], [], []
        for i in (b, b + 1):
            shard = lax.rem(place - offs[i] + shards, shards)
            limits.append((lens[i] - shard * slots) * 4)
            q = q_by_row[i * heads : (i + 1) * heads, :]
            new = new_ref[i].astype(F32)
            key_new = jnp.where(low, new[0:1, :HD], new[0:1, HD:])
            new_values.append(jnp.where(low, new[1:2, :HD], new[1:2, HD:]))
            score_new = jnp.sum(q * key_new, axis=1, keepdims=True) * inv_root
            new_scores.append(jnp.where(place == 0, score_new, -jnp.inf))
            queries.append(q)
        zero = jnp.zeros((heads, HD), F32)
        q = jnp.concatenate(
            [
                jnp.concatenate([queries[0], zero], axis=1),
                jnp.concatenate([zero, queries[1]], axis=1),
            ],
            axis=0,
        ).astype(BF16)
        copies[b].wait()
        copies[b + 1].wait()
        x = jnp.concatenate([buf[b], buf[b + 1]], axis=1)
        raw = lax.dot_general(q, x, (((1,), (1,)), ((), ())), preferred_element_type=F32)
        return x, raw, limits, new_scores, new_values

    ahead = products(0)
    for b in range(0, rows, 2):
        x, raw, limits, new_scores, new_values = ahead
        if b + 2 < rows:
            ahead = products(b + 2)
        left = jnp.where(low, limits[0], limits[1]) - lane
        left = jnp.where((lane & 1) == 0, left, -(1 << 30))
        scores = []
        for c in range(0, width, HD):
            part = raw[:, c : c + HD]
            head0 = jnp.concatenate([part[:group], part[heads : heads + group]], axis=0)
            head1 = jnp.concatenate([part[group:heads], part[heads + group :]], axis=0)
            scores.append(jnp.where(left > c, jnp.where(first, head0, head1), -jnp.inf))
        most = scores[0]
        for part in scores[1:]:
            most = jnp.maximum(most, part)
        tops = []
        for h, mine in enumerate((first, ~first)):
            top = jnp.max(jnp.where(mine, most, -jnp.inf), axis=1, keepdims=True) * inv_root
            new = jnp.concatenate([s[h * group : (h + 1) * group] for s in new_scores], axis=0)
            top = jnp.maximum(jnp.maximum(top, new), -1e30)
            tops.append(top.astype(BF16).astype(F32))
        shift = jnp.where(first, tops[0], tops[1]) * LOG2E
        total = jnp.zeros((2 * group, HD), F32)
        moved = []
        for part in scores:
            weight = jnp.exp2(part * (inv_root * LOG2E) - shift)
            total = total + weight
            moved.append(pltpu.roll(weight, 1, 1))
        moved = [[jnp.where(first, w, 0.0).astype(BF16), jnp.where(first, 0.0, w).astype(BF16)] for w in moved]
        lhs = [
            jnp.concatenate([pair[h][i * group : (i + 1) * group] for pair in moved], axis=1)
            for i in (0, 1)
            for h in (0, 1)
        ]
        summed = jnp.dot(jnp.concatenate(lhs, axis=0), x, preferred_element_type=F32)
        totals = [
            jnp.sum(jnp.where(mine, total, 0.0), axis=1, keepdims=True) for mine in (first, ~first)
        ]
        for i in (0, 1):
            for h in (0, 1):
                mine = slice(i * group, (i + 1) * group)
                theirs = slice(h * group, (h + 1) * group)
                top = tops[h][mine]
                weight_new = jnp.exp(new_scores[i][theirs] - top)
                value = summed[i * heads + h * group :][:group, i * HD : (i + 1) * HD]
                value = value + weight_new.astype(BF16).astype(F32) * new_values[i][theirs]
                block = value.astype(BF16)
                for dest in range(h, out_ref.shape[0], 2):
                    out_ref[dest, (b + i) * group : (b + i + 1) * group, :] = block
                stat = jnp.where(stat_lane == b + i, top, stats[h])
                stats[h] = jnp.where(stat_lane == HALF + b + i, totals[h][mine] + weight_new, stat)
    for h in (0, 1):
        for dest in range(h, out_ref.shape[0], 2):
            out_ref[dest, rows * group :, :] = stats[h].astype(BF16)


def join(parts, rows):
    group = parts[0].shape[0] // (rows + 1)
    stats = [part[rows * group :].astype(F32) for part in parts]
    top = stats[0]
    for stat in stats[1:]:
        top = jnp.maximum(top, stat)
    factors = [jnp.exp(stat - top) for stat in stats]
    total = sum(f * pltpu.roll(stat, HALF, 1) for f, stat in zip(factors, stats))
    sums = []
    for b in range(rows):
        mine = slice(b * group, (b + 1) * group)
        sums.append(sum(part[mine].astype(F32) * f[:, b : b + 1] for part, f in zip(parts, factors)))
    return sums, top, total


def combine_kernel(parts_ref, out_ref):
    parts = [parts_ref[i] for i in range(parts_ref.shape[0])]
    group = 16
    rows = parts_ref.shape[1] // group - 1
    sums, top, total = join(parts, rows)
    stats = jnp.where(lanes(group) < HALF, top, pltpu.roll(total, HALF, 1))
    block = jnp.concatenate(sums + [stats], axis=0).astype(BF16)
    out_ref[...] = jnp.broadcast_to(block[None], out_ref.shape)


def project_kernel(parts_ref, residual_ref, gain_ref, own_ref, theirs_ref, out_ref, attn):
    group = 16
    rows = parts_ref.shape[1] // group - 1
    sums, _, total = join([parts_ref[i] for i in range(parts_ref.shape[0])], rows)
    for b in range(rows):
        attn[b * group : (b + 1) * group, :] = sums[b] / total[:, b : b + 1]
    lhs = jnp.concatenate([attn[pl.ds(g, rows, group), :] for g in range(group)], axis=1).astype(BF16)
    mine = pl.ds(pl.multiple_of(lax.axis_index("core") * (group * HD), group * HD), group * HD)
    own = jnp.dot(lhs, own_ref[mine, :], preferred_element_type=F32)
    theirs = jnp.dot(lhs, theirs_ref[mine, :], preferred_element_type=F32)
    core = lax.axis_index("core")
    total = jnp.concatenate(
        [jnp.where(core == 0, own, theirs), jnp.where(core == 0, theirs, own)], axis=1
    )
    gain = jnp.broadcast_to(gain_ref[...].astype(F32).reshape(1, HD), (rows, HD))
    place = core * lax.axis_size("head") + lax.axis_index("head")
    residual = jnp.concatenate([residual_ref[...].astype(F32)] * (total.shape[1] // HD), axis=1)
    column = lax.broadcasted_iota(jnp.int32, total.shape, 1)
    mine = (column >= place * HD) & (column < place * HD + HD)
    block = jnp.concatenate([total + jnp.where(mine, residual, 0.0), gain], axis=1).astype(BF16)
    out_ref[...] = jnp.broadcast_to(block[None], out_ref.shape)


def stream_kernel(parts_ref, own_ref, out_ref):
    count, rows, width = parts_ref.shape
    width -= HD
    parts = parts_ref[...].astype(F32)
    total = parts[0, :, :width]
    for i in range(1, count):
        total = total + parts[i, :, :width]
    wide = total.astype(BF16).astype(F32)
    gain = jnp.concatenate([parts[i, :, width:] for i in range(count)], axis=1)
    squares = jnp.sum(wide * wide, axis=1, keepdims=True)
    high = squares.astype(BF16).astype(F32)
    tail = jnp.where(lanes(rows) < HALF, high, squares - high)
    block = jnp.concatenate([wide * gain, tail], axis=1).astype(BF16)
    out_ref[...] = jnp.broadcast_to(block[None], out_ref.shape)
    place = lax.axis_index("core") * lax.axis_size("head") + lax.axis_index("head")
    own = wide[:, :HD]
    for i in range(1, count):
        own = jnp.where(place == i, wide[:, i * HD : (i + 1) * HD], own)
    own_ref[...] = own.astype(BF16)


def gated_kernel(x_ref, own_ref, gate_ref, up_ref, stream_ref, out_ref):
    stream_ref[...] = own_ref[...]
    width = x_ref.shape[2] - HD
    tail = x_ref[:, :, width:].astype(F32)
    squares = jnp.sum(tail[:, :, 0:1] + tail[:, :, HALF : HALF + 1], axis=0)
    inv_norm = lax.rsqrt(squares / D + 1e-05)
    lhs = jnp.concatenate([x_ref[i, :, :width] for i in range(x_ref.shape[0])], axis=1)
    gate = jnp.dot(lhs, gate_ref[...], preferred_element_type=F32) * inv_norm
    up = jnp.dot(lhs, up_ref[...], preferred_element_type=F32) * inv_norm
    out_ref[...] = (gate / (1.0 + jnp.exp(-gate)) * up).astype(BF16)


def params(mib):
    return pltpu.CompilerParams(vmem_limit_bytes=mib * MIB)


def kernel_and_exchange():
    return pl.CostEstimate(flops=10**10, bytes_accessed=10**8, transcendentals=0)


def shards(
    queries,
    kv_cache,
    new_kv,
    offsets,
    lengths,
    residual,
    out_weight,
    norm_gain,
    gate_weight,
    up_weight,
):
    rows, slots = kv_cache.shape[:2]
    heads = queries.shape[1] // HD
    group = heads // 2
    ny, nx, nc, nz = (lax.axis_size(name) for name in ALL)
    width = out_weight.shape[1]
    message = rows * group + group
    cache = (
        kv_cache.reshape(rows, slots, 2, 2, HD)
        .transpose(0, 1, 3, 2, 4)
        .reshape(rows, slots * 4, HD)
    )
    parts = pl.pallas_call(
        attention_kernel,
        out_shape=pltpu.VMEM((nx * nc, message, HD), BF16),
        in_specs=[HBM] * 5,
        out_specs=VMEM,
        scratch_shapes=[
            pltpu.SMEM(offsets.shape, jnp.int32),
            pltpu.SMEM(lengths.shape, jnp.int32),
            pltpu.VMEM(queries.shape, BF16),
            pltpu.VMEM(new_kv.shape, BF16),
            pltpu.VMEM(cache.shape, BF16),
            pltpu.VMEM((rows * heads, HD), F32),
            pltpu.SemaphoreType.DMA((rows + 4,)),
        ],
        compiler_params=params(60),
        name="attention",
    )(offsets, lengths, queries, new_kv, cache)
    parts, moving = lax.optimization_barrier((parts, out_weight))
    theirs = lax.ppermute(moving, "core", [(0, 1), (1, 0)])
    parts = lax.all_to_all(parts, ("x", "core"), 0, 0, tiled=True)
    parts, theirs = lax.optimization_barrier((parts, theirs))
    parts = pl.pallas_call(
        combine_kernel,
        out_shape=jax.ShapeDtypeStruct((ny, message, HD), BF16),
        in_specs=[VMEM],
        out_specs=VMEM,
        compiler_params=params(8),
        cost_estimate=kernel_and_exchange(),
        name="combine",
    )(parts)
    parts = lax.all_to_all(parts, "y", 0, 0, tiled=True)
    partial = pl.pallas_call(
        project_kernel,
        out_shape=jax.ShapeDtypeStruct((nc * nz, rows, nc * width + HD), BF16),
        in_specs=[VMEM] * 5,
        out_specs=VMEM,
        scratch_shapes=[pltpu.VMEM((rows * group, HD), F32)],
        compiler_params=params(12),
        name="project",
    )(parts, residual, norm_gain, out_weight, theirs)
    partial = lax.all_to_all(partial, ("core", "head"), 0, 0, tiled=True)
    own, features = pl.pallas_call(
        stream_kernel,
        out_shape=(
            jax.ShapeDtypeStruct((rows, HD), BF16),
            jax.ShapeDtypeStruct((ny * nx, rows, nc * width + HD), BF16),
        ),
        in_specs=[VMEM],
        out_specs=(VMEM, VMEM),
        compiler_params=params(8),
        cost_estimate=kernel_and_exchange(),
        name="stream",
    )(partial)
    features = lax.all_to_all(features, ("y", "x"), 0, 0, tiled=True)
    return pl.pallas_call(
        gated_kernel,
        out_shape=(
            jax.ShapeDtypeStruct((rows, HD), BF16),
            jax.ShapeDtypeStruct((rows, gate_weight.shape[1]), BF16),
        ),
        in_specs=[VMEM] * 4,
        out_specs=(VMEM, VMEM),
        compiler_params=params(24),
        name="gated",
    )(features, own, gate_weight, up_weight)


def solution(mesh):
    split = Mesh(mesh.devices.reshape(4, 4, 2, 4), ALL)
    in_specs = (
        P(None, "head"),
        P(None, KV, None, "head"),
        P(None, None, "head"),
        P(),
        P(),
        P(None, ALL),
        P("head", KV),
        P(ALL),
        P(None, ALL),
        P(None, ALL),
    )
    out_specs = (P(None, ALL), P(None, ALL))
    return jax.shard_map(shards, mesh=split, in_specs=in_specs, out_specs=out_specs, check_vma=False)
```
